32 devices in a mesh: kxy: 8 (over y, x, core), kz: 4 (over z).
Axes of the slice: x: 2, y: 2, z: 4, core: 2. Of those that a mesh axis runs over, the one named last changes fastest.
Arguments:
- factors: float32 [8, 4, 2, 384, 1024], P('kxy', 'kz'), may hold values from -0.9 to 0.9
- occ_energy: float32 [8, 4, 8], P('kxy', 'kz'), may hold values from -2 to -0.5
- vir_energy: float32 [8, 4, 128], P('kxy', 'kz'), may hold values from 0.5 to 3
- shifts: int32 [2, 2], replicated, may hold values from 0 to 3, as said below
Outputs:
- gradient: float32 [8, 4, 2, 384, 1024], P('kxy', 'kz')
The draws below stay inside these ranges and needn't reach their ends.
Inputs may be any that keep to these rules, and one draw needn't show every extreme that they name: `shifts`: row 0 (the momentum transfer) has both entries between 1 and 3. Row 1 is the partner displacement; it is always (3, 3).
All inputs are finite; a program needn't handle non-finite values.
Results may differ from the reference program's by a relative error of at most 0.0001.
Values sent between devices are 32-bit elements; how exact they have to be, the bound alone decides.
A program may use at most 64 MiB of HBM per device.

```python
import jax
import jax.numpy as jnp
from jax import lax

NO = 8
NV = 128
NAUX = 384
REACH = 4
NDISP = 1
NKX = 8
NKZ = 4


def draw_shifts(key, part):
    subkeys = jax.random.split(jax.random.fold_in(key, 17), 4)
    transfer = 1 + jax.random.randint(subkeys[0], (1, 2), 0, REACH - 1)
    displaced = jax.random.randint(subkeys[1], (NDISP, 2), 0, REACH)
    row_first = jax.random.randint(subkeys[2], (), 0, NDISP)
    row_third = jax.random.randint(subkeys[3], (), 0, NDISP)
    displaced = displaced.at[row_first, 0].set(REACH - 1)
    displaced = displaced.at[row_third, 1].set(REACH - 1)
    return jnp.concatenate([transfer, displaced], 0).astype(jnp.int32)


def shard_levels(key, shape, pieces, low, top_value):
    def one(axis_at, blocks):
        draws = jax.random.uniform(jax.random.fold_in(jax.random.fold_in(key, 6), axis_at), (blocks,), jnp.float32, low / len(pieces), top_value / len(pieces))
        return jnp.repeat(jnp.exp(draws), shape[axis_at] // blocks).reshape((-1,) + (1,) * (len(shape) - axis_at - 1))

    loudness = one(*pieces[0])
    for cut in pieces[1:]:
        loudness = loudness * one(*cut)
    return loudness


def noise(own_key, extent, deviation, bound, cuts=(), kind=jnp.bfloat16):
    array = jax.random.normal(own_key, extent, jnp.float32) * deviation
    if len(cuts) > 0:
        array = shard_levels(own_key, extent, cuts, -0.22, 0.18) * array
    return jnp.clip(array, min=-bound, max=bound).astype(kind)


def setup_inputs(seed: int = 0) -> dict:
    key_of = jax.random.split(jax.random.key(seed), 5)
    factors = noise(key_of[0], (NKX, NKZ, 2, NAUX, NO * NV), 0.15, 0.9, ((0, 8), (1, 4)), jnp.float32)
    occ_energy = jnp.clip(-2.0 + 1.5 * jax.random.uniform(key_of[1], (NKX, NKZ, NO), jnp.float32) ** shard_levels(key_of[1], (NKX, NKZ, NO), ((0, 8), (1, 4)), -0.2, 0.2), -2.0, -0.5)
    vir_energy = jnp.clip(0.5 + 2.5 * jax.random.uniform(key_of[2], (NKX, NKZ, NV), jnp.float32) ** shard_levels(key_of[2], (NKX, NKZ, NV), ((0, 8), (1, 4)), -0.2, 0.2), 0.5, 3.0)
    shifts = draw_shifts(jax.random.fold_in(key_of[4], 71), 0)
    return {"factors": factors, "occ_energy": occ_energy, "vir_energy": vir_energy, "shifts": shifts}


def product(left, right):
    return jnp.dot(left, right, precision=lax.Precision.HIGHEST, preferred_element_type=jnp.float32)


def pair_terms(payload):
    own_panel, partner, occ_own, vir_own, occ_part, vir_part = payload
    own_re, own_im = own_panel[0], own_panel[1]
    part_re, part_im = partner[0], partner[1]
    real_v = product(own_re.T, part_re) + product(own_im.T, part_im)
    imag_v = product(own_im.T, part_re) - product(own_re.T, part_im)
    gap_own = (vir_own[None, :] - occ_own[:, None]).reshape(-1)
    gap_part = (vir_part[None, :] - occ_part[:, None]).reshape(-1)
    denominator = gap_own[:, None] + gap_part[None, :]
    real_t = real_v / denominator
    imag_t = imag_v / denominator
    own_grad = jnp.stack([product(part_re, real_t.T) - product(part_im, imag_t.T),
                          product(part_re, imag_t.T) + product(part_im, real_t.T)])
    part_grad = jnp.stack([product(own_re, real_t) + product(own_im, imag_t),
                           product(own_im, real_t) - product(own_re, imag_t)])
    return own_grad, part_grad


def reference(factors, occ_energy, vir_energy, shifts):
    kx_count, kz_count = factors.shape[0], factors.shape[1]
    count = kx_count * kz_count
    vir_used = jnp.roll(vir_energy, (-shifts[0, 0], -shifts[0, 1]), (0, 1))
    gradient_sum = jnp.zeros(factors.shape, jnp.float32)
    flat_panel = factors.reshape((count,) + factors.shape[2:])
    flat_occ = occ_energy.reshape(count, -1)
    flat_vir = vir_used.reshape(count, -1)
    for which_pair in range(NDISP):
        step_x = shifts[which_pair + 1, 0]
        step_z = shifts[which_pair + 1, 1]
        partner = jnp.roll(factors, (-step_x, -step_z), (0, 1)).reshape(flat_panel.shape)
        occ_part = jnp.roll(occ_energy, (-step_x, -step_z), (0, 1)).reshape(flat_occ.shape)
        vir_part = jnp.roll(vir_used, (-step_x, -step_z), (0, 1)).reshape(flat_vir.shape)
        own_grad, part_grad = lax.map(pair_terms, (flat_panel, partner, flat_occ, flat_vir, occ_part, vir_part))
        own_grad = own_grad.reshape(factors.shape)
        part_grad = part_grad.reshape(factors.shape)
        gradient_sum = gradient_sum + own_grad + jnp.roll(part_grad, (step_x, step_z), (0, 1))
    return -gradient_sum
```

```python
import jax
import jax.numpy as jnp
from jax import lax
from jax.sharding import PartitionSpec as P

REACH = 4
CHUNKS = 4
HIGH = lax.Precision.HIGH


def moved(x, by_x, by_z):
    count_x, count_z = lax.axis_size("kxy"), lax.axis_size("kz")
    pairs = []
    for at_x in range(count_x):
        for at_z in range(count_z):
            to_x, to_z = (at_x + by_x) % count_x, (at_z + by_z) % count_z
            pairs.append((at_x * count_z + at_z, to_x * count_z + to_z))
    return lax.ppermute(x, ("kxy", "kz"), pairs)


def shifted(x, axis, by):
    size = lax.axis_size(axis)
    return lax.ppermute(x, axis, [(i, (i + by) % size) for i in range(size)])


def dot(left, right, left_dim, right_dim):
    return lax.dot_general(
        left,
        right,
        (((left_dim,), (right_dim,)), ((), ())),
        precision=HIGH,
        preferred_element_type=jnp.float32,
    )


def amplitudes(first, second, gap_first, gap_second):
    real_v = dot(first[0], second[0], 0, 0) + dot(first[1], second[1], 0, 0)
    imag_v = dot(first[1], second[0], 0, 0) - dot(first[0], second[1], 0, 0)
    scale = 1.0 / (gap_first[:, None] + gap_second[None, :])
    return real_v * scale, imag_v * scale


def gaps(vir, occ):
    return (vir[None, :] - occ[:, None]).reshape(-1)


def body(factors, occ_energy, vir_energy, shifts):
    own = factors[0, 0]
    width = own.shape[2] // CHUNKS
    pieces = [own[:, :, c * width : (c + 1) * width] for c in range(CHUNKS)]
    partner = [moved(piece, 1 - REACH, 1 - REACH) for piece in pieces]
    behind = [moved(piece, REACH - 1, REACH - 1) for piece in pieces]
    vir_moved = vir_energy[0, 0]
    for axis, by in (("kxy", shifts[0, 0]), ("kz", shifts[0, 1])):
        for level in range((REACH - 1).bit_length()):
            arrived = shifted(vir_moved, axis, -(1 << level))
            vir_moved = jnp.where(by >> level & 1 == 1, arrived, vir_moved)
    levels = jnp.concatenate([vir_moved, occ_energy[0, 0]])
    ahead_levels = moved(levels, 1 - REACH, 1 - REACH)
    behind_levels = moved(levels, REACH - 1, REACH - 1)
    virs = vir_moved.shape[0]
    gap_own = gaps(vir_moved, occ_energy[0, 0])
    gap_ahead = gaps(ahead_levels[:virs], ahead_levels[virs:])
    gap_behind = gaps(behind_levels[:virs], behind_levels[virs:])
    real, imag = 0.0, 0.0
    for c in range(CHUNKS):
        here = slice(c * width, (c + 1) * width)
        part = partner[c]
        real_t, imag_t = amplitudes(own, part, gap_own, gap_ahead[here])
        real += dot(part[0], real_t, 1, 1) - dot(part[1], imag_t, 1, 1)
        imag += dot(part[0], imag_t, 1, 1) + dot(part[1], real_t, 1, 1)
        back = behind[c]
        real_t, imag_t = amplitudes(back, own, gap_behind[here], gap_own)
        real += dot(back[0], real_t, 1, 0) + dot(back[1], imag_t, 1, 0)
        imag += dot(back[1], real_t, 1, 0) - dot(back[0], imag_t, 1, 0)
    return -jnp.stack([real, imag])[None, None]


def solution(mesh):
    placed = (P("kxy", "kz", None, None, None), P("kxy", "kz", None), P("kxy", "kz", None), P())
    return jax.shard_map(
        body,
        mesh=mesh,
        in_specs=placed,
        out_specs=P("kxy", "kz", None, None, None),
        check_vma=False,
    )
```

```python
import functools

import jax
import jax.numpy as jnp
from jax import lax
from jax.experimental import pallas as pl
from jax.experimental.pallas import tpu as pltpu
from jax.sharding import PartitionSpec as P

REACH = 4
WINDOW = 2
TILE = 256
MESH = pl.DeviceIdType.MESH


def halves(x):
    high = x.astype(jnp.bfloat16)
    return high, (x - high.astype(jnp.float32)).astype(jnp.bfloat16)


def dot(left, right):
    return jnp.dot(left, right, preferred_element_type=jnp.float32)


def three_pass(left, right):
    return dot(left[0], right[0]) + dot(left[0], right[1]) + dot(left[1], right[0])


def offsets(size_x, size_z):
    reach = range(1, REACH)
    found = set()
    for sign in (1, -1):
        found.update((sign * s % size_x, 0) for s in reach)
        found.update((0, sign * s % size_z) for s in reach)
        found.add((sign * (REACH - 1) % size_x, sign * (REACH - 1) % size_z))
    return sorted(found)


def kernel(
    size_x, size_z, shifts_ref, panel_ref, vir_ref, occ_ref, out_ref,
    landed, own_f32, own_split, mixed, mixed_t, vir_x, vir_step, vir_z, gap_own, gap_landed, gap_column,
    load_sem, send_sem, recv_sem, hop_send, hop_recv, gap_send, gap_recv,
):
    at_x, at_z = lax.axis_index("kxy"), lax.axis_index("kz")
    naux = panel_ref.shape[1]
    occs, virs = occ_ref.shape
    step = REACH - 1

    load = pltpu.make_async_copy(panel_ref, own_f32, load_sem)
    load.start()

    def device(by_x, by_z):
        return (lax.rem(at_x + by_x + size_x * REACH, size_x), lax.rem(at_z + by_z + size_z * REACH, size_z))

    barrier = pltpu.get_barrier_semaphore()
    greeted = offsets(size_x, size_z)
    for by_x, by_z in greeted:
        pl.semaphore_signal(barrier, inc=1, device_id=device(by_x, by_z), device_id_type=MESH)
    pl.semaphore_wait(barrier, len(greeted))

    def hop(source, slots, axis, s):
        return pltpu.make_async_remote_copy(
            src_ref=source,
            dst_ref=slots.at[s - 1],
            send_sem=hop_send.at[axis, s - 1],
            recv_sem=hop_recv.at[axis, s - 1],
            device_id=device(-s, 0) if axis == 0 else device(0, -s),
            device_id_type=MESH,
        )

    def block_copy(way, c):
        sign = 2 * way - 1
        columns = pl.ds(pl.multiple_of(c * virs, virs), virs)
        return pltpu.make_async_remote_copy(
            src_ref=panel_ref.at[:, :, columns],
            dst_ref=landed.at[way, :, :, columns],
            send_sem=send_sem.at[way, c],
            recv_sem=recv_sem.at[way, c],
            device_id=device(sign * step, sign * step),
            device_id_type=MESH,
        )

    def gap_copy(way):
        sign = 2 * way - 1
        return pltpu.make_async_remote_copy(
            src_ref=gap_own,
            dst_ref=gap_landed.at[way],
            send_sem=gap_send.at[way],
            recv_sem=gap_recv.at[way],
            device_id=device(sign * step, sign * step),
            device_id_type=MESH,
        )

    for s in range(1, REACH):
        hop(vir_ref, vir_x, 0, s).start()
    for c in range(WINDOW):
        for way in range(2):
            block_copy(way, c).start()

    def chosen(slots, by):
        picked = slots[0]
        for s in range(2, REACH):
            picked = jnp.where(by == s, slots[s - 1], picked)
        return picked

    for s in range(1, REACH):
        hop(vir_ref, vir_x, 0, s).wait()
    vir_step[...] = chosen(vir_x, shifts_ref[0, 0])
    for s in range(1, REACH):
        hop(vir_step, vir_z, 1, s).start()
    load.wait()
    for part in range(2):
        rows = pl.ds(part * naux, naux)
        for at in range(0, own_split.shape[2], TILE):
            high, low = halves(own_f32[part, :, at : at + TILE])
            own_split[0, rows, at : at + TILE] = high
            own_split[1, rows, at : at + TILE] = low
    out_ref[...] = jnp.zeros_like(out_ref)
    for s in range(1, REACH):
        hop(vir_step, vir_z, 1, s).wait()
    gap_own[...] = chosen(vir_z, shifts_ref[0, 1]) - occ_ref[...]
    for way in range(2):
        gap_copy(way).start()
    for way in range(2):
        gap_copy(way).wait()
        for i in range(occs):
            row = gap_landed[way, i : i + 1, :]
            gap_column[way, i] = jnp.broadcast_to(row, (virs, virs)).T

    def work(at, carry):
        c, way = lax.div(at, 2), lax.rem(at, 2)

        @pl.when(way == 0)
        def _():
            for each in range(2):
                block_copy(each, c).wait_send()

            @pl.when(c + WINDOW < occs)
            def _():
                for each in range(2):
                    block_copy(each, c + WINDOW).start()

        block_copy(way, c).wait_recv()
        columns = pl.ds(pl.multiple_of(c * virs, virs), virs)
        real = landed[way, 0, :, columns]
        imag = landed[way, 1, :, columns]
        for which, (r, i) in enumerate(zip(halves(real), halves(imag))):
            mixed[which, :naux, :virs] = r
            mixed[which, :naux, virs:] = -i
            mixed[which, naux:, :virs] = i
            mixed[which, naux:, virs:] = r
        for which, (r, i) in enumerate(zip(halves(real.T), halves(imag.T))):
            mixed_t[which, :virs, :naux] = r
            mixed_t[which, :virs, naux:] = i
            mixed_t[which, virs:, :naux] = -i
            mixed_t[which, virs:, naux:] = r
        column_gap = gap_column[way, c]
        for start in range(0, occs * virs, TILE):
            tile = slice(start, start + TILE)
            v = three_pass((mixed_t[0], mixed_t[1]), (own_split[0, :, tile], own_split[1, :, tile]))
            scale = jnp.concatenate(
                [1.0 / (column_gap + gap_own[j : j + 1, :]) for j in range(start // virs, (start + TILE) // virs)], 1
            )
            t = halves(v * jnp.concatenate([scale, scale], 0))
            out_ref[:, tile] += three_pass((mixed[0], mixed[1]), t)
        return carry

    lax.fori_loop(0, 2 * occs, work, 0)


def body(factors, occ_energy, vir_energy, shifts):
    size_x, size_z = lax.axis_size("kxy"), lax.axis_size("kz")
    panel = factors[0, 0]
    parts, naux, pairs = panel.shape
    occs, virs = occ_energy.shape[2], vir_energy.shape[2]
    vir_rows = jnp.broadcast_to(vir_energy[0, 0][None, :], (occs, virs))
    occ_rows = jnp.broadcast_to(occ_energy[0, 0][:, None], (occs, virs))
    f32, bf16, dma = jnp.float32, jnp.bfloat16, pltpu.SemaphoreType.DMA
    vmem = pl.BlockSpec(memory_space=pltpu.VMEM)
    total = pl.pallas_call(
        functools.partial(kernel, size_x, size_z),
        out_shape=jax.ShapeDtypeStruct((parts * naux, pairs), f32),
        in_specs=[pl.BlockSpec(memory_space=pltpu.SMEM), pl.BlockSpec(memory_space=pl.ANY), vmem, vmem],
        out_specs=vmem,
        scratch_shapes=[
            pltpu.VMEM((2, parts, naux, pairs), f32),
            pltpu.VMEM((parts, naux, pairs), f32),
            pltpu.VMEM((2, parts * naux, pairs), bf16),
            pltpu.VMEM((2, parts * naux, 2 * virs), bf16),
            pltpu.VMEM((2, 2 * virs, parts * naux), bf16),
            pltpu.VMEM((REACH - 1, occs, virs), f32),
            pltpu.VMEM((occs, virs), f32),
            pltpu.VMEM((REACH - 1, occs, virs), f32),
            pltpu.VMEM((occs, virs), f32),
            pltpu.VMEM((2, occs, virs), f32),
            pltpu.VMEM((2, occs, virs, virs), f32),
            dma,
            dma((2, occs)),
            dma((2, occs)),
            dma((2, REACH - 1)),
            dma((2, REACH - 1)),
            dma((2,)),
            dma((2,)),
        ],
        compiler_params=pltpu.CompilerParams(
            collective_id=0, has_side_effects=True, vmem_limit_bytes=48 * 1024 * 1024
        ),
        cost_estimate=pl.CostEstimate(
            flops=48 * naux * pairs * pairs, bytes_accessed=8 * panel.size, transcendentals=0
        ),
    )(shifts, panel, vir_rows, occ_rows)
    return -total.reshape(1, 1, parts, naux, pairs)


def solution(mesh):
    placed = (P("kxy", "kz", None, None, None), P("kxy", "kz", None), P("kxy", "kz", None), P())
    return jax.shard_map(
        body,
        mesh=mesh,
        in_specs=placed,
        out_specs=P("kxy", "kz", None, None, None),
        check_vma=False,
    )
```

```python
import functools

import jax
import jax.numpy as jnp
from jax import lax
from jax.experimental import pallas as pl
from jax.experimental.pallas import tpu as pltpu
from jax.sharding import PartitionSpec as P

REACH = 4
WINDOW = 2
TILE = 256
MESH = pl.DeviceIdType.MESH


def halves(x):
    high = x.astype(jnp.bfloat16)
    return high, (x - high.astype(jnp.float32)).astype(jnp.bfloat16)


def dot(left, right):
    return jnp.dot(left, right, preferred_element_type=jnp.float32)


def three_pass(left, right):
    return dot(left[0], right[0]) + dot(left[0], right[1]) + dot(left[1], right[0])


def offsets(size_x, size_z):
    reach = range(1, REACH)
    found = set()
    for sign in (1, -1):
        found.update((sign * s % size_x, 0) for s in reach)
        found.update((0, sign * s % size_z) for s in reach)
        found.add((sign * (REACH - 1) % size_x, sign * (REACH - 1) % size_z))
    return sorted(found)


def kernel(
    size_x, size_z, shifts_ref, panel_ref, vir_ref, occ_ref, out_ref,
    landed, own_f32, own_split, mixed, mixed_t, vir_own, vir_x, vir_step, vir_z, gap_own, gap_landed, gap_column,
    load_sem, send_sem, recv_sem, hop_send, hop_recv, gap_send, gap_recv,
):
    at_x, at_z = lax.axis_index("kxy"), lax.axis_index("kz")
    naux = panel_ref.shape[1]
    occs, virs = gap_own.shape
    step = REACH - 1

    def load(c):
        return pltpu.make_async_copy(panel_ref.at[:, :, c * virs : (c + 1) * virs], own_f32.at[c], load_sem.at[c])

    for c in range(occs):
        load(c).start()
    vir_own[...] = jnp.broadcast_to(vir_ref[...], (occs, virs))

    def device(by_x, by_z):
        return (lax.rem(at_x + by_x + size_x * REACH, size_x), lax.rem(at_z + by_z + size_z * REACH, size_z))

    barrier = pltpu.get_barrier_semaphore()
    greeted = offsets(size_x, size_z)
    for by_x, by_z in greeted:
        pl.semaphore_signal(barrier, inc=1, device_id=device(by_x, by_z), device_id_type=MESH)
    pl.semaphore_wait(barrier, len(greeted))

    def hop(source, slots, axis, s):
        return pltpu.make_async_remote_copy(
            src_ref=source,
            dst_ref=slots.at[s - 1],
            send_sem=hop_send.at[axis, s - 1],
            recv_sem=hop_recv.at[axis, s - 1],
            device_id=device(-s, 0) if axis == 0 else device(0, -s),
            device_id_type=MESH,
        )

    def block_copy(way, c):
        sign = 2 * way - 1
        return pltpu.make_async_remote_copy(
            src_ref=own_f32.at[c],
            dst_ref=landed.at[way, c],
            send_sem=send_sem.at[way, c],
            recv_sem=recv_sem.at[way, c],
            device_id=device(sign * step, sign * step),
            device_id_type=MESH,
        )

    def gap_copy(way):
        sign = 2 * way - 1
        return pltpu.make_async_remote_copy(
            src_ref=gap_own,
            dst_ref=gap_landed.at[way],
            send_sem=gap_send.at[way],
            recv_sem=gap_recv.at[way],
            device_id=device(sign * step, sign * step),
            device_id_type=MESH,
        )

    for s in range(1, REACH):
        hop(vir_own, vir_x, 0, s).start()
    for c in range(WINDOW):
        load(c).wait()
        for way in range(2):
            block_copy(way, c).start()

    def chosen(slots, by):
        picked = slots[0]
        for s in range(2, REACH):
            picked = jnp.where(by == s, slots[s - 1], picked)
        return picked

    for s in range(1, REACH):
        hop(vir_own, vir_x, 0, s).wait()
    vir_step[...] = chosen(vir_x, shifts_ref[0, 0])
    for s in range(1, REACH):
        hop(vir_step, vir_z, 1, s).start()
    for c in range(WINDOW, occs):
        load(c).wait()
    for c in range(occs):
        columns = slice(c * virs, (c + 1) * virs)
        for part in range(2):
            rows = slice(part * naux, (part + 1) * naux)
            high, low = halves(own_f32[c, part])
            own_split[0, rows, columns] = high
            own_split[1, rows, columns] = low
    out_ref[...] = jnp.zeros_like(out_ref)
    for s in range(1, REACH):
        hop(vir_step, vir_z, 1, s).wait()
    vir_used = chosen(vir_z, shifts_ref[0, 1])
    for i in range(occs):
        gap_own[i : i + 1, :] = vir_used[i : i + 1, :] - occ_ref[0, i]
    for way in range(2):
        gap_copy(way).start()
    for way in range(2):
        gap_copy(way).wait()
        for i in range(occs):
            row = gap_landed[way, i : i + 1, :]
            gap_column[way, i] = jnp.broadcast_to(row, (virs, virs)).T

    def work(at, carry):
        c, way = lax.div(at, 2), lax.rem(at, 2)

        @pl.when(way == 0)
        def _():
            for each in range(2):
                block_copy(each, c).wait_send()

            @pl.when(c + WINDOW < occs)
            def _():
                for each in range(2):
                    block_copy(each, c + WINDOW).start()

        block_copy(way, c).wait_recv()
        real = landed[way, c, 0]
        imag = landed[way, c, 1]
        for which, (r, i) in enumerate(zip(halves(real), halves(imag))):
            mixed[which, :naux, :virs] = r
            mixed[which, :naux, virs:] = -i
            mixed[which, naux:, :virs] = i
            mixed[which, naux:, virs:] = r
        for which, (r, i) in enumerate(zip(halves(real.T), halves(imag.T))):
            mixed_t[which, :virs, :naux] = r
            mixed_t[which, :virs, naux:] = i
            mixed_t[which, virs:, :naux] = -i
            mixed_t[which, virs:, naux:] = r
        column_gap = gap_column[way, c]
        for start in range(0, occs * virs, TILE):
            tile = slice(start, start + TILE)
            v = three_pass((mixed_t[0], mixed_t[1]), (own_split[0, :, tile], own_split[1, :, tile]))
            scale = jnp.concatenate(
                [1.0 / (column_gap + gap_own[j : j + 1, :]) for j in range(start // virs, (start + TILE) // virs)], 1
            )
            t = halves(v * jnp.concatenate([scale, scale], 0))
            out_ref[:, tile] += three_pass((mixed[0], mixed[1]), t)
        return carry

    lax.fori_loop(0, 2 * occs, work, 0)


def body(factors, occ_energy, vir_energy, shifts):
    size_x, size_z = lax.axis_size("kxy"), lax.axis_size("kz")
    panel = factors[0, 0]
    parts, naux, pairs = panel.shape
    occs, virs = occ_energy.shape[2], vir_energy.shape[2]
    f32, bf16, dma = jnp.float32, jnp.bfloat16, pltpu.SemaphoreType.DMA
    smem = pl.BlockSpec(memory_space=pltpu.SMEM)
    vmem = pl.BlockSpec(memory_space=pltpu.VMEM)
    total = pl.pallas_call(
        functools.partial(kernel, size_x, size_z),
        out_shape=jax.ShapeDtypeStruct((parts * naux, pairs), f32),
        in_specs=[smem, pl.BlockSpec(memory_space=pl.ANY), vmem, smem],
        out_specs=vmem,
        scratch_shapes=[
            pltpu.VMEM((2, occs, parts, naux, virs), f32),
            pltpu.VMEM((occs, parts, naux, virs), f32),
            pltpu.VMEM((2, parts * naux, pairs), bf16),
            pltpu.VMEM((2, parts * naux, 2 * virs), bf16),
            pltpu.VMEM((2, 2 * virs, parts * naux), bf16),
            pltpu.VMEM((occs, virs), f32),
            pltpu.VMEM((REACH - 1, occs, virs), f32),
            pltpu.VMEM((occs, virs), f32),
            pltpu.VMEM((REACH - 1, occs, virs), f32),
            pltpu.VMEM((occs, virs), f32),
            pltpu.VMEM((2, occs, virs), f32),
            pltpu.VMEM((2, occs, virs, virs), f32),
            dma((occs,)),
            dma((2, occs)),
            dma((2, occs)),
            dma((2, REACH - 1)),
            dma((2, REACH - 1)),
            dma((2,)),
            dma((2,)),
        ],
        compiler_params=pltpu.CompilerParams(
            collective_id=0, has_side_effects=True, vmem_limit_bytes=48 * 1024 * 1024
        ),
        cost_estimate=pl.CostEstimate(
            flops=48 * naux * pairs * pairs, bytes_accessed=8 * panel.size, transcendentals=0
        ),
    )(shifts, panel, vir_energy[0], occ_energy[0])
    return -total.reshape(1, 1, parts, naux, pairs)


def solution(mesh):
    placed = (P("kxy", "kz", None, None, None), P("kxy", "kz", None), P("kxy", "kz", None), P())
    return jax.shard_map(
        body,
        mesh=mesh,
        in_specs=placed,
        out_specs=P("kxy", "kz", None, None, None),
        check_vma=False,
    )
```

```python
import functools

import jax
import jax.numpy as jnp
from jax import lax
from jax.experimental import pallas as pl
from jax.experimental.pallas import tpu as pltpu
from jax.sharding import PartitionSpec as P

REACH = 4
WINDOW = 2
TILE = 256
MESH = pl.DeviceIdType.MESH


def halves(x):
    high = x.astype(jnp.bfloat16)
    return high, (x - high.astype(jnp.float32)).astype(jnp.bfloat16)


def dot(left, right):
    return jnp.dot(left, right, preferred_element_type=jnp.float32)


def three_pass(left, right):
    return dot(left[0], right[0]) + dot(left[0], right[1]) + dot(left[1], right[0])


def offsets(size_x, size_z):
    reach = range(1, REACH)
    found = set()
    for sign in (1, -1):
        found.update((sign * s % size_x, 0) for s in reach)
        found.update((0, sign * s % size_z) for s in reach)
        found.add((sign * (REACH - 1) % size_x, sign * (REACH - 1) % size_z))
    return sorted(found)


def kernel(
    size_x, size_z, shifts_ref, panel_ref, vir_ref, occ_ref, out_ref,
    landed, own_f32, own_split, mixed, mixed_t, vir_own, vir_x, vir_step, vir_z, gap_own, gap_landed, gap_column,
    load_sem, send_sem, recv_sem, hop_send, hop_recv, gap_send, gap_recv,
):
    at_x, at_z = lax.axis_index("kxy"), lax.axis_index("kz")
    naux = panel_ref.shape[1]
    occs, virs = gap_own.shape
    step = REACH - 1

    def load(c):
        return pltpu.make_async_copy(panel_ref.at[:, :, c * virs : (c + 1) * virs], own_f32.at[c], load_sem.at[c])

    for c in range(occs):
        load(c).start()
    vir_own[...] = jnp.broadcast_to(vir_ref[...], (occs, virs))

    def device(by_x, by_z):
        return (lax.rem(at_x + by_x + size_x * REACH, size_x), lax.rem(at_z + by_z + size_z * REACH, size_z))

    barrier = pltpu.get_barrier_semaphore()
    greeted = offsets(size_x, size_z)
    for by_x, by_z in greeted:
        pl.semaphore_signal(barrier, inc=1, device_id=device(by_x, by_z), device_id_type=MESH)
    pl.semaphore_wait(barrier, len(greeted))

    def hop(source, slots, axis, s):
        return pltpu.make_async_remote_copy(
            src_ref=source,
            dst_ref=slots.at[s - 1],
            send_sem=hop_send.at[axis, s - 1],
            recv_sem=hop_recv.at[axis, s - 1],
            device_id=device(-s, 0) if axis == 0 else device(0, -s),
            device_id_type=MESH,
        )

    def block_copy(way, c):
        sign = 2 * way - 1
        return pltpu.make_async_remote_copy(
            src_ref=own_f32.at[c],
            dst_ref=landed.at[way, c],
            send_sem=send_sem.at[way, c],
            recv_sem=recv_sem.at[way, c],
            device_id=device(sign * step, sign * step),
            device_id_type=MESH,
        )

    def gap_copy(way):
        sign = 2 * way - 1
        return pltpu.make_async_remote_copy(
            src_ref=gap_own,
            dst_ref=gap_landed.at[way],
            send_sem=gap_send.at[way],
            recv_sem=gap_recv.at[way],
            device_id=device(sign * step, sign * step),
            device_id_type=MESH,
        )

    for s in range(1, REACH):
        hop(vir_own, vir_x, 0, s).start()
    for c in range(WINDOW):
        load(c).wait()
        block_copy(0, c).start()

    def chosen(slots, by):
        picked = slots[0]
        for s in range(2, REACH):
            picked = jnp.where(by == s, slots[s - 1], picked)
        return picked

    for s in range(1, REACH):
        hop(vir_own, vir_x, 0, s).wait()
    vir_step[...] = chosen(vir_x, shifts_ref[0, 0])
    for s in range(1, REACH):
        hop(vir_step, vir_z, 1, s).start()
    for c in range(WINDOW, occs):
        load(c).wait()
    for c in range(occs):
        columns = slice(c * virs, (c + 1) * virs)
        for part in range(2):
            rows = slice(part * naux, (part + 1) * naux)
            high, low = halves(own_f32[c, part])
            own_split[0, rows, columns] = high
            own_split[1, rows, columns] = low
    out_ref[...] = jnp.zeros_like(out_ref)
    for s in range(1, REACH):
        hop(vir_step, vir_z, 1, s).wait()
    vir_used = chosen(vir_z, shifts_ref[0, 1])
    for i in range(occs):
        gap_own[i : i + 1, :] = vir_used[i : i + 1, :] - occ_ref[0, i]
    for way in range(2):
        gap_copy(way).start()
    for c in range(WINDOW):
        block_copy(1, c).start()
    for way in range(2):
        gap_copy(way).wait()
        for i in range(occs):
            row = gap_landed[way, i : i + 1, :]
            gap_column[way, i] = jnp.broadcast_to(row, (virs, virs)).T

    def work(at, carry):
        c, way = lax.div(at, 2), lax.rem(at, 2)

        block_copy(way, c).wait_send()

        @pl.when(c + WINDOW < occs)
        def _():
            block_copy(way, c + WINDOW).start()

        block_copy(way, c).wait_recv()
        real = landed[way, c, 0]
        imag = landed[way, c, 1]
        for which, (r, i) in enumerate(zip(halves(real), halves(imag))):
            mixed[which, :naux, :virs] = r
            mixed[which, :naux, virs:] = -i
            mixed[which, naux:, :virs] = i
            mixed[which, naux:, virs:] = r
        for which, (r, i) in enumerate(zip(halves(real.T), halves(imag.T))):
            mixed_t[which, :virs, :naux] = r
            mixed_t[which, :virs, naux:] = i
            mixed_t[which, virs:, :naux] = -i
            mixed_t[which, virs:, naux:] = r
        column_gap = gap_column[way, c]
        for start in range(0, occs * virs, TILE):
            tile = slice(start, start + TILE)
            v = three_pass((mixed_t[0], mixed_t[1]), (own_split[0, :, tile], own_split[1, :, tile]))
            scale = jnp.concatenate(
                [1.0 / (column_gap + gap_own[j : j + 1, :]) for j in range(start // virs, (start + TILE) // virs)], 1
            )
            t = halves(v * jnp.concatenate([scale, scale], 0))
            out_ref[:, tile] += three_pass((mixed[0], mixed[1]), t)
        return carry

    lax.fori_loop(0, 2 * occs, work, 0)


def body(factors, occ_energy, vir_energy, shifts):
    size_x, size_z = lax.axis_size("kxy"), lax.axis_size("kz")
    panel = factors[0, 0]
    parts, naux, pairs = panel.shape
    occs, virs = occ_energy.shape[2], vir_energy.shape[2]
    f32, bf16, dma = jnp.float32, jnp.bfloat16, pltpu.SemaphoreType.DMA
    smem = pl.BlockSpec(memory_space=pltpu.SMEM)
    vmem = pl.BlockSpec(memory_space=pltpu.VMEM)
    total = pl.pallas_call(
        functools.partial(kernel, size_x, size_z),
        out_shape=jax.ShapeDtypeStruct((parts * naux, pairs), f32),
        in_specs=[smem, pl.BlockSpec(memory_space=pl.ANY), vmem, smem],
        out_specs=vmem,
        scratch_shapes=[
            pltpu.VMEM((2, occs, parts, naux, virs), f32),
            pltpu.VMEM((occs, parts, naux, virs), f32),
            pltpu.VMEM((2, parts * naux, pairs), bf16),
            pltpu.VMEM((2, parts * naux, 2 * virs), bf16),
            pltpu.VMEM((2, 2 * virs, parts * naux), bf16),
            pltpu.VMEM((occs, virs), f32),
            pltpu.VMEM((REACH - 1, occs, virs), f32),
            pltpu.VMEM((occs, virs), f32),
            pltpu.VMEM((REACH - 1, occs, virs), f32),
            pltpu.VMEM((occs, virs), f32),
            pltpu.VMEM((2, occs, virs), f32),
            pltpu.VMEM((2, occs, virs, virs), f32),
            dma((occs,)),
            dma((2, occs)),
            dma((2, occs)),
            dma((2, REACH - 1)),
            dma((2, REACH - 1)),
            dma((2,)),
            dma((2,)),
        ],
        compiler_params=pltpu.CompilerParams(
            collective_id=0, has_side_effects=True, vmem_limit_bytes=48 * 1024 * 1024
        ),
        cost_estimate=pl.CostEstimate(
            flops=48 * naux * pairs * pairs, bytes_accessed=8 * panel.size, transcendentals=0
        ),
    )(shifts, panel, vir_energy[0], occ_energy[0])
    return -total.reshape(1, 1, parts, naux, pairs)


def solution(mesh):
    placed = (P("kxy", "kz", None, None, None), P("kxy", "kz", None), P("kxy", "kz", None), P())
    return jax.shard_map(
        body,
        mesh=mesh,
        in_specs=placed,
        out_specs=P("kxy", "kz", None, None, None),
        check_vma=False,
    )
```
